32 devices in a mesh: redist: 16 (over z, y, x), contract: 2 (over core).
Axes of the slice: x: 2, y: 2, z: 4, core: 2. Of those that a mesh axis runs over, the one named last changes fastest.
Arguments:
- amps: float32 [6400, 128, 128], P('redist', None, 'contract'), may hold values from -6 to 6
- integrals: float32 [80, 128, 16, 128], P(None, 'contract'), may hold values from -0.3125 to 0.3125
- occ_irrep: int32 [80], replicated, may hold values from 0 to 7
- block_sizes: int32 [8], replicated, may hold values from 1 to 128, 800 in all
- slot_order: int32 [128], replicated, may hold values from 0 to 127, each once
- occ_energy: float32 [80], replicated, may hold values from -3 to -0.5
- vir_energy: float32 [8, 128], replicated, may hold values from 0.3 to 3
Outputs:
- update: float32 [80, 128, 16, 128], P(None, 'redist', None, 'contract')
The draws below stay inside these ranges and needn't reach their ends.
Inputs may be any that keep to these rules, and one draw needn't show every extreme that they name: `block_sizes`: block sizes of the 8 occupied irreps sum to 800; the largest is 128. `slot_order`: each slot appears once.
All inputs are finite; a program needn't handle non-finite values.
Results may differ from the reference program's by a relative error of at most 0.00007.
Values sent between devices are 32-bit elements; how exact they have to be, the bound alone decides.
A program may use at most 192 MiB of HBM per device.

```python
import math
import jax
import jax.numpy as jnp
import numpy as np
from jax import lax

NO = 80
NV = 800
VB = 128
IRREPS = 8
JS = 16
PAIRS = 6400


def touch_ends(array, key, smallest, top_value):
    longest = array.shape.index(max(array.shape))
    spots = []
    for shift in (0, 1):
        where = [jax.random.randint(jax.random.fold_in(key, axis), (), 0, length) for axis, length in enumerate(array.shape)]
        where[longest] = (where[longest] + shift) % array.shape[longest]
        spots.append(tuple(where))
    return array.at[spots[0]].set(smallest).at[spots[1]].set(top_value)


def with_spikes(result, own_key, source, target, parts, factor):
    def block_of(dim):
        return (jnp.arange(result.shape[dim]) // (result.shape[dim] // parts)).reshape((-1,) + (1,) * (result.ndim - 1 - dim))

    near = jax.random.permutation(own_key, parts)[block_of(target)]
    second = (block_of(target) + parts // 2) % parts
    return jnp.where((block_of(source) == near) | (block_of(source) == second), factor * result, result)


def level_of(rng, dims, shards, smallest, high):
    def one(position, blocks):
        heights = jax.random.uniform(jax.random.fold_in(jax.random.fold_in(rng, 6), position), (blocks,), jnp.float32, smallest / len(shards), high / len(shards))
        return jnp.repeat(jnp.exp(heights), dims[position] // blocks).reshape((-1,) + (1,) * (len(dims) - position - 1))

    loudness = one(*shards[0])
    for cut in shards[1:]:
        loudness = loudness * one(*cut)
    return loudness


def profile(number_of, total, bound, slope):
    portions = [(1 << 20) // math.isqrt(standing ** slope) + 1 for standing in range(2, number_of + 1)]
    surplus, given = total - bound - (number_of - 1), [1] * (number_of - 1)
    while surplus > 0:
        free = [i for i in range(number_of - 1) if given[i] < bound]
        pool, left = sum([portions[i] for i in free]), surplus
        for i in free:
            addition = min(bound - given[i], max(1, left * portions[i] // pool), surplus)
            given[i] = given[i] + addition
            surplus = surplus - addition
    return np.array([bound] + given)


def uneven_parts(rng, amount, total, most, lean):
    if amount == 2:
        one = jax.random.randint(rng, (), max(1, total - most), min(most, total - 1) + 1)
        return jnp.stack([one, total - one])
    tallies = jnp.asarray(profile(amount, total, most, lean), jnp.int32)
    couples = (amount - 1) // 2
    donor, taker = tallies[1:1 + 2 * couples:2], tallies[2:2 + 2 * couples:2]
    margin = jnp.minimum(donor - 1, most - taker)
    shifted = jax.random.randint(jax.random.fold_in(rng, 1), (couples,), 0, 1 << 20) % (margin + 1)
    tallies = tallies.at[1:1 + 2 * couples:2].set(donor - shifted).at[2:2 + 2 * couples:2].set(taker + shifted)
    return tallies[jax.random.permutation(jax.random.fold_in(rng, 2), amount)]


def centred(stream_key, extent, scale, reach, pieces=(), held_as=jnp.bfloat16):
    entries = scale * jax.random.normal(stream_key, extent, jnp.float32)
    if pieces:
        entries = entries * level_of(stream_key, extent, pieces, -0.22, 0.18)
    return jnp.clip(entries, -reach, reach).astype(held_as)


def heavy_noise(key, dims, spread, most, cuts, heavy, kind=jnp.bfloat16):
    values = spread * jax.random.normal(key, dims, jnp.float32)
    if cuts:
        values = values * level_of(key, dims, cuts, -0.22, 0.18)
    return jnp.clip(with_spikes(values, jax.random.fold_in(key, 3), *heavy), -most, most).astype(kind)


def setup_inputs(seed: int = 0) -> dict:
    seeds = jax.random.split(jax.random.key(seed), 8)
    return {
        "amps": centred(seeds[0], (PAIRS, VB, VB), 1.0, 6.0, ((0, 16), (2, 2)), jnp.float32),
        "integrals": heavy_noise(seeds[1], (NO, VB, JS, VB), (NO * VB // 16) ** -0.5, 0.3125, ((1, 2),), (1, 3, 2, 2.0), jnp.float32),
        "occ_irrep": touch_ends(jax.random.randint(seeds[2], (NO,), 0, IRREPS), jax.random.fold_in(seeds[2], 1), 0, IRREPS - 1).astype(jnp.int32),
        "block_sizes": uneven_parts(seeds[3], IRREPS, NV, VB, 2).astype(jnp.int32),
        "slot_order": jax.random.permutation(seeds[4], VB).astype(jnp.int32),
        "occ_energy": jnp.clip(jax.random.uniform(seeds[5], (NO,), jnp.float32, -3.0, -0.5), -3.0, -0.5),
        "vir_energy": jnp.clip(jax.random.uniform(seeds[6], (IRREPS, VB), jnp.float32, 0.3, 3.0), 0.3, 3.0),
    }


def reference(amps, integrals, occ_irrep, block_sizes, slot_order, occ_energy, vir_energy):
    labels = jnp.arange(IRREPS, dtype=jnp.int32)
    hits = occ_irrep[:, None] == labels[None, :]
    occ_limit = jnp.sum(jnp.where(hits, block_sizes[None, :], 0), axis=1).astype(jnp.int32)
    slots = jnp.arange(VB, dtype=jnp.int32)
    blocks = amps.reshape(NO, NO, VB, VB)
    keep_kc = slots[None, :] < occ_limit[:, None]
    masked = jnp.where(keep_kc[:, None, None, :], blocks, jnp.zeros((), blocks.dtype))
    cycle = jnp.einsum("kiac,kcjb->iajb", masked, integrals, precision=lax.Precision.HIGHEST,
                      preferred_element_type=jnp.float32)
    cycle = jnp.take(cycle, slot_order, axis=1)
    row_energy = jnp.take(vir_energy[occ_irrep], slot_order, axis=1)
    col_energy = vir_energy[occ_irrep[:JS]]
    denom = (row_energy[:, :, None, None] + col_energy[None, None, :, :]) - occ_energy[:, None, None, None] - occ_energy[:JS][None, None, :, None]
    keep_row = slot_order[None, :] < occ_limit[:, None]
    keep_col = slots[None, :] < occ_limit[:JS][:, None]
    keep = keep_row[:, :, None, None] & keep_col[None, None, :, :]
    return jnp.where(keep, cycle / denom, jnp.zeros((), cycle.dtype))
```

```python
import functools
import jax
import jax.numpy as jnp
from jax import lax
from jax.experimental import pallas as pl
from jax.experimental.pallas import tpu as pltpu
from jax.sharding import PartitionSpec as P

MESH = pl.DeviceIdType.MESH
PLANE = 4
LAYERS = 4


def split(x):
    hi = x.astype(jnp.bfloat16)
    return hi, (x - hi.astype(jnp.float32)).astype(jnp.bfloat16)


def regroup_kernel(x_ref, first_ref, second_ref, out_ref):
    pair, _, group, share, lanes = x_ref.shape
    rows = pair * share
    inner = []
    for high in range(PLANE):
        wide = jnp.concatenate(
            [x_ref[:, 0, high * LAYERS + low].reshape(rows, lanes) for low in range(LAYERS)], axis=1
        )
        both = jnp.concatenate(split(wide), axis=0)
        inner.append(
            jnp.dot(both, first_ref[...], preferred_element_type=jnp.float32).astype(jnp.bfloat16)
        )
    for layer in range(LAYERS):
        wide = jnp.concatenate([one[:, layer * lanes:(layer + 1) * lanes] for one in inner], axis=1)
        picked = jnp.dot(wide, second_ref[...], preferred_element_type=jnp.float32)
        picked = picked[:rows] + picked[rows:]
        for mate in range(PLANE):
            out_ref[mate, 0, layer] = picked[:, mate * lanes:(mate + 1) * lanes]


def cycle_kernel(
    a_ref, hi_ref, lo_ref, out_ref,
    got, x_hi, x_lo, part, both, near, far,
    own_sem, swap_send, swap_recv, core_send, core_recv, near_send, near_recv, far_send, far_recv,
):
    groups = a_ref.shape[1]
    rows = a_ref.shape[3]
    lanes = a_ref.shape[4]
    full = hi_ref.shape[0]
    half = full // 2
    me = lax.axis_index("redist")
    core = lax.axis_index("contract")
    layer, mate = me // PLANE, me % PLANE
    mate_y, mate_x = mate // 2, mate % 2
    mates = [((mate_y + d // 2) % 2) * 2 + (mate_x + d % 2) % 2 for d in range(PLANE)]
    beside = layer + 1 - 2 * (layer % 2)
    across = (layer + 2) % LAYERS
    beyond = (beside + 2) % LAYERS
    other = 1 - core

    barrier = pltpu.get_barrier_semaphore()
    partners = [(layer * PLANE + mates[d], core) for d in range(1, PLANE)]
    partners += [(me, other), (beside * PLANE + mate, core), (across * PLANE + mate, core)]
    for partner in partners:
        pl.semaphore_signal(barrier, inc=1, device_id=partner, device_id_type=MESH)
    pl.semaphore_wait(barrier, len(partners))

    def own(g):
        return pltpu.make_async_copy(a_ref.at[mate, g], got.at[g, 0], own_sem.at[g])

    def remote(src, dst, send, recv, device):
        return pltpu.make_async_remote_copy(
            src_ref=src, dst_ref=dst, send_sem=send, recv_sem=recv,
            device_id=device, device_id_type=MESH,
        )

    def swap(g, d):
        return remote(a_ref.at[mates[d], g], got.at[g, d], swap_send.at[g, d - 1],
                      swap_recv.at[g, d - 1], (layer * PLANE + mates[d], core))

    def cores(g):
        return remote(part.at[g % 2, :, pl.ds(other * half, half), :], both.at[g],
                      core_send.at[g], core_recv.at[g], (me, other))

    def nearby(g, n):
        block = beyond if n else beside
        return remote(both.at[g, block], near.at[g, n], near_send.at[g, n],
                      near_recv.at[g, n], (beside * PLANE + mate, core))

    def away(g):
        return remote(both.at[g, across], far.at[g], far_send.at[g], far_recv.at[g],
                      (across * PLANE + mate, core))

    def begin(g):
        for d in (3, 1, 2):
            swap(g, d).start()
        own(g).start()

    def multiply(g):
        for d in range(PLANE):
            def cast(b, carry, d=d):
                at = pl.ds(d * rows, rows)
                hi, lo = split(got[g, d, b])
                x_hi[b, at, :] = hi
                x_lo[b, at, :] = lo
                return carry
            lax.fori_loop(0, LAYERS, cast, 0)
        tile = full // 8

        def step(m, carry):
            at = pl.ds(pl.multiple_of(m * tile, tile), tile)
            w_hi, w_lo = hi_ref[at, :], lo_ref[at, :]
            for b in range(0, LAYERS, 2):
                xh = jnp.concatenate([x_hi[b], x_hi[b + 1]], axis=1)
                xl = jnp.concatenate([x_lo[b], x_lo[b + 1]], axis=1)
                total = jnp.dot(w_hi, xh, preferred_element_type=jnp.float32)
                total += jnp.dot(w_hi, xl, preferred_element_type=jnp.float32)
                total += jnp.dot(w_lo, xh, preferred_element_type=jnp.float32)
                part[g % 2, b, at, :] = total[:, :lanes]
                part[g % 2, b + 1, at, :] = total[:, lanes:]
            return carry
        lax.fori_loop(0, 8, step, 0)

    begin(0)
    if groups > 1:
        begin(1)
    for g in range(groups + 1):
        if g < groups:
            own(g).wait()
            for d in (1, 2, 3):
                swap(g, d).wait_recv()
            if g + 2 < groups:
                begin(g + 2)
            if g >= 2:
                cores(g - 2).wait_send()
            multiply(g)
            cores(g).start()
        if g >= 1:
            nearby(g - 1, 1).wait_recv()
            both[g - 1, across] = both[g - 1, across] + near[g - 1, 1]
            away(g - 1).start()
        if g < groups:
            cores(g).wait_recv()

            def add(b, carry, g=g):
                at = pl.ds(pl.multiple_of(core * half, half), half)
                both[g, b] = both[g, b] + part[g % 2, b, at, :]
                return carry
            lax.fori_loop(0, LAYERS, add, 0)
            nearby(g, 1).start()
            nearby(g, 0).start()
    for g in range(groups):
        nearby(g, 0).wait_recv()
        away(g).wait_recv()
        out_ref[g] = (both[g, layer] + near[g, 0]) + far[g]
    for g in range(groups):
        for d in range(1, PLANE):
            swap(g, d).wait_send()
        if g >= groups - 2:
            cores(g).wait_send()
        nearby(g, 0).wait_send()
        nearby(g, 1).wait_send()
        away(g).wait_send()


def fast_cycle(amps, integrals, occ_limit, slot_order, col_ids):
    redist_count = lax.axis_size("redist")
    occ_total = occ_limit.shape[0]
    share = amps.shape[2]
    lanes = amps.shape[1]
    slab, columns = integrals.shape[2:]
    slot_dev = lanes // redist_count
    per = redist_count
    pair = amps.shape[0] // occ_total
    groups = occ_total // per
    rows = pair * share
    full = slab * columns
    depth = PLANE * rows
    wide = LAYERS * lanes

    me = lax.axis_index("redist")
    layer, mate = me // PLANE, me % PLANE
    mate_y, mate_x = mate // 2, mate % 2

    chosen = (slot_order.reshape(LAYERS, PLANE, slot_dev)[None] ==
              jnp.arange(lanes, dtype=jnp.int32)[:, None, None, None])
    same = jnp.eye(LAYERS, dtype=jnp.bool_)
    first = (chosen[None, :, :, None, :, :] & same[:, None, None, :, None, None])
    first = first.reshape(wide, wide).astype(jnp.bfloat16)
    old = jnp.arange(wide, dtype=jnp.int32)
    target = ((old // slot_dev) % PLANE) * lanes + (old // (slot_dev * PLANE)) * slot_dev + old % slot_dev
    second = (target[:, None] == old[None, :]).astype(jnp.bfloat16)

    x = jnp.transpose(amps, (0, 2, 1)).reshape(pair, groups, per, share, lanes)
    ordered = pl.pallas_call(
        regroup_kernel,
        grid=(groups,),
        out_shape=jax.ShapeDtypeStruct((PLANE, groups, LAYERS, rows, lanes), jnp.float32),
        in_specs=[
            pl.BlockSpec((pair, 1, per, share, lanes), lambda g: (0, g, 0, 0, 0)),
            pl.BlockSpec((wide, wide), lambda g: (0, 0)),
            pl.BlockSpec((wide, wide), lambda g: (0, 0)),
        ],
        out_specs=pl.BlockSpec((PLANE, 1, LAYERS, rows, lanes), lambda g: (0, g, 0, 0, 0)),
        compiler_params=pltpu.CompilerParams(vmem_limit_bytes=48 * 2**20),
        name="regroup",
    )(x, first, second)

    slabs, limits = [], []
    for d in range(PLANE):
        mate_d = ((mate_y + d // 2) % 2) * 2 + (mate_x + d % 2) % 2
        at = (layer * PLANE + mate_d) * pair
        slabs.append(lax.dynamic_slice_in_dim(integrals, at, pair, 0))
        limits.append(lax.dynamic_slice_in_dim(occ_limit, at, pair, 0))
    w = jnp.concatenate(slabs, axis=0)
    keep = col_ids[None, :] < jnp.concatenate(limits)[:, None]
    w = jnp.where(keep[:, :, None, None], w, jnp.zeros((), w.dtype))
    w = w.reshape(PLANE * pair, share, slab, 2, columns // 2)
    w = jnp.transpose(w, (3, 2, 4, 0, 1)).reshape(full, depth)
    w_top = lax.reduce_precision(w, 8, 7)
    w_hi = w_top.astype(jnp.bfloat16)
    w_lo = (w - w_top).astype(jnp.bfloat16)

    vmem = pl.BlockSpec(memory_space=pltpu.VMEM)
    dma = pltpu.SemaphoreType.DMA
    out = pl.pallas_call(
        cycle_kernel,
        out_shape=jax.ShapeDtypeStruct((groups, full // 2, lanes), jnp.float32),
        in_specs=[pl.BlockSpec(memory_space=pl.ANY), vmem, vmem],
        out_specs=vmem,
        scratch_shapes=[
            pltpu.VMEM((groups, PLANE, LAYERS, rows, lanes), jnp.float32),
            pltpu.VMEM((LAYERS, depth, lanes), jnp.bfloat16),
            pltpu.VMEM((LAYERS, depth, lanes), jnp.bfloat16),
            pltpu.VMEM((2, LAYERS, full, lanes), jnp.float32),
            pltpu.VMEM((groups, LAYERS, full // 2, lanes), jnp.float32),
            pltpu.VMEM((groups, 2, full // 2, lanes), jnp.float32),
            pltpu.VMEM((groups, full // 2, lanes), jnp.float32),
            dma((groups,)),
            dma((groups, PLANE - 1)), dma((groups, PLANE - 1)),
            dma((groups,)), dma((groups,)),
            dma((groups, 2)), dma((groups, 2)),
            dma((groups,)), dma((groups,)),
        ],
        compiler_params=pltpu.CompilerParams(
            collective_id=0, has_side_effects=True, vmem_limit_bytes=60 * 2**20
        ),
        cost_estimate=pl.CostEstimate(
            flops=6 * full * depth * groups * wide,
            bytes_accessed=4 * depth * groups * wide,
            transcendentals=0,
        ),
        name="cycle",
    )(ordered, w_hi, w_lo)
    out = out.reshape(groups, slab, columns // 2, per, slot_dev)
    return jnp.transpose(out, (0, 3, 4, 1, 2)).reshape(occ_total, slot_dev, slab, columns // 2)


def plain_cycle(amps, integrals, occ_limit, slot_order, col_ids):
    redist_count = lax.axis_size("redist")
    occ_total = occ_limit.shape[0]
    share = integrals.shape[1]
    slot_dev = slot_order.shape[0] // redist_count
    ordered = jnp.take(amps, slot_order, axis=1)
    moved = lax.all_to_all(ordered, "redist", split_axis=1, concat_axis=0, tiled=True)
    blocks = moved.reshape(occ_total, occ_total, slot_dev, share)
    keep_kc = col_ids[None, :] < occ_limit[:, None]
    masked = jnp.where(keep_kc[:, None, None, :], blocks, jnp.zeros((), blocks.dtype))
    summed = lax.psum_scatter(
        jnp.einsum(
            "kiac,kcjb->biaj",
            masked,
            integrals,
            precision=lax.Precision.HIGHEST,
            preferred_element_type=jnp.float32,
        ),
        "contract",
        scatter_dimension=0,
        tiled=True,
    )
    return jnp.transpose(summed, (1, 2, 3, 0))


def per_device(amps, integrals, occ_irrep, block_sizes, slot_order, occ_energy, vir_energy):
    redist_count = lax.axis_size("redist")
    occ_total = occ_irrep.shape[0]
    slab = integrals.shape[2]
    share = integrals.shape[1]
    irrep_total = vir_energy.shape[0]
    slot_total = vir_energy.shape[1]
    slot_dev = slot_total // redist_count
    labels = jnp.arange(irrep_total, dtype=jnp.int32)
    hits = occ_irrep[:, None] == labels[None, :]
    occ_limit = jnp.sum(jnp.where(hits, block_sizes[None, :], 0), axis=1)
    col_first = lax.axis_index("contract") * share
    col_ids = col_first + jnp.arange(share, dtype=jnp.int32)
    fits = (
        redist_count == PLANE * LAYERS
        and lax.axis_size("contract") == 2
        and amps.shape[0] % occ_total == 0
        and occ_total % redist_count == 0
        and slot_total == 128
        and slot_dev % 8 == 0
    )
    form = fast_cycle if fits else plain_cycle
    cycle = form(amps, integrals, occ_limit, slot_order, col_ids)
    my_slots = lax.dynamic_slice_in_dim(
        slot_order, lax.axis_index("redist") * slot_dev, slot_dev, 0
    )
    mine = my_slots[:, None] == jnp.arange(slot_total, dtype=jnp.int32)[None, :]
    vir_rows = jnp.sum(
        jnp.where(mine[None], vir_energy[:, None, :], jnp.zeros((), vir_energy.dtype)), axis=2
    )
    row_energy = jnp.sum(
        jnp.where(hits[:, :, None], vir_rows[None, :, :], jnp.zeros((), vir_rows.dtype)), axis=1
    )
    vir_cols = lax.dynamic_slice_in_dim(vir_energy, col_first, share, 1)
    col_energy = jnp.sum(
        jnp.where(hits[:slab, :, None], vir_cols[None, :, :], jnp.zeros((), vir_cols.dtype)), axis=1
    )
    denom = (
        row_energy[:, :, None, None]
        + col_energy[None, None, :, :]
        - occ_energy[:, None, None, None]
        - occ_energy[:slab][None, None, :, None]
    )
    keep_row = my_slots[None, :] < occ_limit[:, None]
    keep_col = col_ids[None, :] < occ_limit[:slab][:, None]
    keep = keep_row[:, :, None, None] & keep_col[None, None, :, :]
    return jnp.where(keep, cycle / denom, jnp.zeros((), cycle.dtype))


def solution(mesh):
    placed = (
        P("redist", None, "contract"),
        P(None, "contract", None, None),
        P(),
        P(),
        P(),
        P(),
        P(),
    )
    return jax.shard_map(
        per_device,
        mesh=mesh,
        in_specs=placed,
        out_specs=P(None, "redist", None, "contract"),
        check_vma=False,
    )
```
